128 devices in a mesh: fft: 64 (over y_hi, x, z, core), grp: 2 (over y_lo).
Axes of the slice: x: 4, y: 4 (y_hi: 2, y_lo: 2; y = y_hi * 2 + y_lo), z: 4, core: 2. Of those that a mesh axis runs over, the one named last changes fastest.
Arguments:
- limbs_a: int32 [4096, 8192], P(('fft', 'grp')), may hold values from -128 to 127
- limbs_b: int32 [4096, 8192], P(('fft', 'grp')), may hold values from -128 to 127
Outputs:
- product: float32 [4096, 16384], P(('fft', 'grp'))
The draws below stay inside these ranges and needn't reach their ends.
All inputs are finite; a program needn't handle non-finite values.
Results may differ from the reference program's by a relative error of at most 0.000098.
Values sent between devices are 32-bit elements; how exact they have to be, the bound alone decides.
A program may use at most 128 MiB of HBM per device.

```python
import jax
import jax.numpy as jnp
from jax import lax

ROWS = 16384
COLS = 4096


def set_ends(drawn, own_key, low, high):
    index_at = [jax.random.randint(jax.random.fold_in(own_key, axis), (), 0, length) for axis, length in enumerate(drawn.shape)]
    main_axis = drawn.shape.index(max(drawn.shape))
    neighbour = index_at[:main_axis] + [(index_at[main_axis] + 1) % drawn.shape[main_axis]] + index_at[main_axis + 1:]
    return drawn.at[tuple(index_at)].set(low).at[tuple(neighbour)].set(high)


def setup_inputs(seed: int = 0) -> dict:
    keys = jax.random.split(jax.random.key(seed), 3)
    return {
        "limbs_a": set_ends(jax.random.randint(keys[0], (COLS, ROWS // 2), -128, 128), jax.random.fold_in(keys[0], 1), -128, 127).astype(jnp.int32),
        "limbs_b": set_ends(jax.random.randint(keys[1], (COLS, ROWS // 2), -128, 128), jax.random.fold_in(keys[1], 1), -128, 127).astype(jnp.int32),
    }


def reference(limbs_a, limbs_b):
    padding = jnp.zeros(limbs_a.shape, jnp.float32)
    digits_a = jnp.concatenate([limbs_a.astype(jnp.float32), padding], axis=1).T.reshape(-1)
    digits_b = jnp.concatenate([limbs_b.astype(jnp.float32), padding], axis=1).T.reshape(-1)
    signal = lax.complex(digits_a, digits_b)
    spectrum = jnp.fft.fft(signal)
    mirror = jnp.conj(jnp.roll(jnp.flip(spectrum), 1))
    first_part = (spectrum + mirror) * 0.5
    second_part = (spectrum - mirror) * (-0.5j)
    pointwise = first_part * second_part
    total = ROWS * COLS
    coeffs = jnp.real(jnp.fft.ifft(pointwise)) * total
    out_scale = 1.0 / (total * 5461.25 * ((total // 2) ** 0.5))
    return (coeffs * out_scale).reshape(ROWS, COLS).T
```

```python
import functools
import math

import jax
import jax.numpy as jnp
import ml_dtypes
import numpy as np
from jax import lax
from jax.experimental import pallas as pl
from jax.experimental.pallas import tpu as pltpu
from jax.sharding import PartitionSpec as P

MESH = pl.DeviceIdType.MESH
ROWS = 16384
COLS = 4096
TOTAL = ROWS * COLS
DIGIT_VAR = 5461.25
DEV = 128
LOCAL = COLS // DEV
FWD_CHUNKS = 4
INV_CHUNKS = 2
F32 = jnp.float32
BF16 = jnp.bfloat16


def turn(num, den):
    angle = (np.asarray(num, np.int64) % den) * (2.0 * math.pi / den)
    return np.cos(angle), np.sin(angle)


def split_pair(table):
    high = table.astype(ml_dtypes.bfloat16)
    low = (table - high.astype(np.float64)).astype(ml_dtypes.bfloat16)
    return high, low


@functools.lru_cache(None)
def matrix_tables():
    ka = np.arange(128)
    lane = np.arange(64)
    order = np.concatenate([2 * np.arange(64), 2 * np.arange(64) + 1])
    c, s = turn(np.outer(2 * ka + 1, order), 512)
    first = split_pair(np.concatenate([c, -s], 0))
    first = np.concatenate([first[0], first[1]], 1)
    c, s = turn(np.outer(lane, lane), 64)
    z = np.zeros_like(c)
    c2, s2 = np.block([[c, z], [z, c]]), np.block([[s, z], [z, s]])
    lanes_fwd = split_pair(np.block([[c2, -s2], [s2, c2]]))
    lanes_inv = split_pair(np.block([[c2, s2], [-s2, c2]]))
    c, s = turn(np.outer(ka, ka), 128)
    dev_fwd = split_pair(np.block([[c, s], [-s, c]]))
    dev_inv = split_pair(np.block([[c, -s], [s, c]]))
    scale = 2.0 / (TOTAL * DIGIT_VAR * math.sqrt(TOTAL // 2))
    order = np.concatenate([2 * np.arange(128), 2 * np.arange(128) + 1])
    c, s = turn(np.outer(order, 2 * ka + 1), 512)
    last = split_pair(np.concatenate([c, -s], 1) * scale)
    mats = [first, *lanes_fwd, *dev_fwd, *dev_inv, *lanes_inv, *last]
    return np.stack(mats)


@functools.lru_cache(None)
def vector_tables():
    ka = np.arange(128)[:, None]
    lane = np.arange(128)[None, :]
    low, par = lane % 64, lane // 64
    zero = 0 * lane
    k1 = ka + 256 * low
    pairs = [
        turn(-low * (2 * ka + 1), 2 * ROWS),
        turn(-(2 * k1 + 1), 2 * TOTAL),
        turn(-ka + zero, COLS),
        turn(ka * par, COLS),
        turn(2 * ka + zero, COLS),
        turn(2 * (2 * k1 + 1), 2 * TOTAL),
        turn(par * (2 * k1 + 1), 2 * TOTAL),
        turn(np.arange(128)[:, None] % 16 * par, 32),
    ]
    return np.stack([t for pair in pairs for t in pair]).astype(np.float32)


def times(a, b):
    return a[0] * b[0] - a[1] * b[1], a[0] * b[1] + a[1] * b[0]


def turned(value, num, den):
    num %= den
    re, im = value
    if num == 0:
        return value
    if 4 * num == den:
        return -im, re
    if 2 * num == den:
        return -re, -im
    if 4 * num == 3 * den:
        return im, -re
    c, s = math.cos(2 * math.pi * num / den), math.sin(2 * math.pi * num / den)
    if 8 * num % den == 0:
        root = math.sqrt(0.5)
        sc, ss = math.copysign(1.0, c), math.copysign(1.0, s)
        first = re if sc > 0 else -re
        first = first - im if ss > 0 else first + im
        second = re if ss > 0 else -re
        second = second + im if sc > 0 else second - im
        return first * root, second * root
    return re * c - im * s, re * s + im * c


def small_dft(values, sign):
    n = len(values)
    if n == 1:
        return values
    half = n // 2
    even = [(a[0] + b[0], a[1] + b[1]) for a, b in zip(values[:half], values[half:])]
    odd = [
        turned((a[0] - b[0], a[1] - b[1]), sign * i, n)
        for i, (a, b) in enumerate(zip(values[:half], values[half:]))
    ]
    even, odd = small_dft(even, sign), small_dft(odd, sign)
    return [v for pair in zip(even, odd) for v in pair]


def halves(value):
    high = value.astype(BF16)
    return high, (value - high.astype(F32)).astype(BF16)


def dot(a, b):
    return jnp.dot(a, b, preferred_element_type=F32)


def kernel(
    a_hbm, b_hbm, mats_hbm, vecs_hbm, out_hbm,
    a_ref, b_ref, mats, vecs, out_ref, sent, got, mid, quot, back, home, turn_f, turn_d,
    in_sem, out_sem, send_f, recv_f, send_i, recv_i,
):
    me = lax.axis_index("fft") * 2 + lax.axis_index("grp")
    barrier = pltpu.get_barrier_semaphore()

    loads = [
        pltpu.make_async_copy(src, dst, in_sem.at[i])
        for i, (src, dst) in enumerate(
            ((a_hbm, a_ref), (b_hbm, b_ref), (mats_hbm, mats), (vecs_hbm, vecs))
        )
    ]
    for load in loads:
        load.start()

    def greet(step, _):
        peer = lax.rem(me + step, DEV)
        pl.semaphore_signal(
            barrier, inc=1, device_id=(peer // 2, lax.rem(peer, 2)), device_id_type=MESH
        )
        return 0

    lax.fori_loop(1, DEV, greet, 0)

    def peer_at(step):
        mixed = lax.rem(step * 37, DEV)
        core = lax.rem(me // 2 + mixed, 2)
        x = lax.rem(me // 16 + mixed // 2, 4)
        y = lax.rem((me // 64) * 2 + lax.rem(me, 2) + mixed // 8, 4)
        z = lax.rem(me // 4 + mixed // 32, 4)
        return (y // 2) * 64 + x * 16 + z * 4 + core * 2 + lax.rem(y, 2)

    def scatter(src, dst, first, count, send_sem, recv_sem):
        part = pl.ds(first, count)
        pltpu.make_async_copy(
            src.at[part, :, pl.ds(me, 1)], dst.at[part, :, pl.ds(me, 1)], recv_sem
        ).start()

        def send(step, _):
            peer = peer_at(step)
            pltpu.make_async_remote_copy(
                src_ref=src.at[part, :, pl.ds(peer, 1)],
                dst_ref=dst.at[part, :, pl.ds(me, 1)],
                send_sem=send_sem,
                recv_sem=recv_sem,
                device_id=(peer // 2, lax.rem(peer, 2)),
                device_id_type=MESH,
            ).start()
            return 0

        lax.fori_loop(1, DEV, send, 0)

    def arrived(src, dst, first, count, recv_sem):
        part = pl.ds(first, count)
        pltpu.make_async_copy(src.at[part], dst.at[part], recv_sem).wait()

    def all_sent(src, dst, send_sem):
        part = pl.ds(0, DEV - 1)
        pltpu.make_async_copy(src.at[:, :, part], dst.at[:, :, part], send_sem).wait()

    for load in loads:
        load.wait()

    row = lax.broadcasted_iota(jnp.int32, (128, 128), 0)
    lane = lax.broadcasted_iota(jnp.int32, (128, 128), 1)
    left = lane < 64
    odd_bin = 2 * (row + 256 * lax.rem(lane, 64)) + 1
    angle = (me * odd_bin).astype(F32) * (2.0 * math.pi / (2 * TOTAL // LOCAL))
    own = (jnp.cos(angle), -jnp.sin(angle))
    turn_f[0], turn_f[1] = own
    turn_d[0] = jnp.ones((128, 128), F32)
    turn_d[1] = jnp.zeros((128, 128), F32)
    tw = lambda i: (vecs[2 * i], vecs[2 * i + 1])

    per_f = LOCAL // FWD_CHUNKS

    def forward(g, _):
        for pair in range(0, 8, 2):
            cols = []
            for cs in (pair, pair + 1):
                a = a_ref[g, pl.ds(cs, 64, stride=8), :].astype(F32)
                b = b_ref[g, pl.ds(cs, 64, stride=8), :].astype(F32)
                lo = jnp.where(left[:64], a, pltpu.roll(b, 64, 1))
                hi = jnp.where(left[:64], pltpu.roll(a, 64, 1), b)
                cols.append(jnp.concatenate([lo, hi], 0).astype(BF16))
            x = jnp.concatenate(cols, 1)
            u = dot(mats[0], jnp.concatenate([x, x], 0))
            rows = []
            for i in range(2):
                v = times((u[:128, 128 * i : 128 * i + 128], u[128:, 128 * i : 128 * i + 128]), tw(0))
                rows.append(jnp.concatenate(v, 1))
            vh, vl = halves(jnp.concatenate(rows, 0))
            y = dot(vh, mats[1]) + dot(vl, mats[1]) + dot(vh, mats[2])
            for i in range(2):
                t = (turn_f[0], turn_f[1])
                r = times((y[128 * i : 128 * i + 128, :128], y[128 * i : 128 * i + 128, 128:]), t)
                sent[8 * g + pair + i, 0] = r[0]
                sent[8 * g + pair + i, 1] = r[1]
                turn_f[0], turn_f[1] = times(t, tw(1))

        @pl.when(g == 0)
        def _():
            pl.semaphore_wait(barrier, DEV - 1)

        scatter(sent, got, 8 * g, 8, send_f, recv_f.at[g])
        return 0

    lax.fori_loop(0, FWD_CHUNKS, forward, 0)

    def devices_digit(g, _):
        arrived(sent, got, 8 * g, 8, recv_f.at[g])
        for part in range(0, 8, 4):
            first = 8 * g + part
            x = jnp.concatenate([got[first + i].reshape(256, 128) for i in range(4)], 1)
            xh, xl = halves(x)
            y = dot(mats[3], xh) + dot(mats[3], xl) + dot(mats[4], xh)
            for i in range(4):
                t = (turn_d[0], turn_d[1])
                r = times((y[:128, 128 * i : 128 * i + 128], y[128:, 128 * i : 128 * i + 128]), t)
                mid[first + i, 0] = r[0]
                mid[first + i, 1] = r[1]
                turn_d[0], turn_d[1] = times(t, tw(2))
        return 0

    lax.fori_loop(0, FWD_CHUNKS, devices_digit, 0)

    lane8 = lax.broadcasted_iota(jnp.int32, (8, 128), 1)
    sign = jnp.where(lane8 < 64, 1.0, -1.0).astype(F32)

    def product(t, _):
        rows = pl.ds(pl.multiple_of(8 * t, 8), 8)
        bins = small_dft([(mid[i, 0, rows, :], mid[i, 1, rows, :]) for i in range(LOCAL)], -1)
        prod = []
        for x in bins:
            y = (pltpu.roll(x[0], 64, 1), pltpu.roll(x[1], 64, 1))
            prod.append(times(x, y))
        folded = []
        for i in range(16):
            p, q = prod[i], prod[i + 16]
            f = (p[0] + sign * q[0], p[1] + sign * q[1])
            w = (vecs[14, pl.ds(i, 1), :], vecs[15, pl.ds(i, 1), :])
            folded.append(times(f, w))
        for i, v in enumerate(small_dft(folded, 1)):
            quot[i, 0, rows, :] = v[0]
            quot[i, 1, rows, :] = v[1]
        return 0

    lax.fori_loop(0, 16, product, 0)

    turn_d[0], turn_d[1] = tw(3)
    per_i = 4 // INV_CHUNKS

    def devices_back(chunk, _):
        for part in range(per_i):
            first = 4 * (chunk * per_i + part)
            cols = []
            for i in range(4):
                t = (turn_d[0], turn_d[1])
                r = times((quot[first + i, 0], quot[first + i, 1]), t)
                cols.append(jnp.concatenate(r, 0))
                turn_d[0], turn_d[1] = times(t, tw(4))
            xh, xl = halves(jnp.concatenate(cols, 1))
            y = dot(mats[5], xh) + dot(mats[5], xl) + dot(mats[6], xh)
            for i in range(4):
                back[first + i, 0] = y[:128, 128 * i : 128 * i + 128]
                back[first + i, 1] = y[128:, 128 * i : 128 * i + 128]
        scatter(back, home, 4 * chunk * per_i, 4 * per_i, send_i, recv_i.at[chunk])
        return 0

    lax.fori_loop(0, INV_CHUNKS, devices_back, 0)

    turn_f[0], turn_f[1] = times((own[0], -own[1]), tw(6))

    def inverse(g, _):
        @pl.when(lax.rem(g, per_i) == 0)
        def _():
            arrived(back, home, 4 * g, 4 * per_i, recv_i.at[g // per_i])

        for pair in range(0, 4, 2):
            rows = []
            for i in range(2):
                t = (turn_f[0], turn_f[1])
                at = 4 * g + pair + i
                rows.append(jnp.concatenate(times((home[at, 0], home[at, 1]), t), 1))
                turn_f[0], turn_f[1] = times(t, tw(5))
            xh, xl = halves(jnp.concatenate(rows, 0))
            v = dot(xh, mats[7]) + dot(xl, mats[7]) + dot(xh, mats[8])
            c, s = tw(0)
            cols = []
            for i in range(2):
                vi = times((v[128 * i : 128 * i + 128, :128], v[128 * i : 128 * i + 128, 128:]), (c, -s))
                cols.append(jnp.concatenate(vi, 0))
            vh, vl = halves(jnp.concatenate(cols, 1))
            o = dot(mats[9], vh) + dot(mats[9], vl) + dot(mats[10], vh)
            for i in range(2):
                o0, o1 = o[:128, 128 * i : 128 * i + 128], o[128:, 128 * i : 128 * i + 128]
                cs = 2 * (pair + i)
                out_ref[g, pl.ds(cs, 128, stride=8), :] = jnp.where(left, o0, pltpu.roll(o1, 64, 1))
                out_ref[g, pl.ds(cs + 1, 128, stride=8), :] = jnp.where(left, pltpu.roll(o0, 64, 1), o1)
        pltpu.make_async_copy(out_ref.at[g], out_hbm.at[g], out_sem).start()
        return 0

    lax.fori_loop(0, 4, inverse, 0)
    pltpu.make_async_copy(out_ref, out_hbm, out_sem).wait()
    all_sent(sent, got, send_f)
    all_sent(back, home, send_i)


def on_device(limbs_a, limbs_b):
    def tiles(x):
        return x.reshape(4, 8, 64, 128).transpose(0, 2, 1, 3).reshape(4, 512, 128)

    out = pl.pallas_call(
        kernel,
        out_shape=jax.ShapeDtypeStruct((4, 1024, 128), F32),
        in_specs=[pl.BlockSpec(memory_space=pl.ANY)] * 4,
        out_specs=pl.BlockSpec(memory_space=pl.ANY),
        scratch_shapes=[
            pltpu.VMEM((4, 512, 128), jnp.int32),
            pltpu.VMEM((4, 512, 128), jnp.int32),
            pltpu.VMEM((11, 256, 256), BF16),
            pltpu.VMEM((16, 128, 128), F32),
            pltpu.VMEM((4, 1024, 128), F32),
            pltpu.VMEM((LOCAL, 2, 128, 128), F32),
            pltpu.VMEM((LOCAL, 2, 128, 128), F32),
            pltpu.VMEM((LOCAL, 2, 128, 128), F32),
            pltpu.VMEM((16, 2, 128, 128), F32),
            pltpu.VMEM((16, 2, 128, 128), F32),
            pltpu.VMEM((16, 2, 128, 128), F32),
            pltpu.VMEM((2, 128, 128), F32),
            pltpu.VMEM((2, 128, 128), F32),
            pltpu.SemaphoreType.DMA((4,)),
            pltpu.SemaphoreType.DMA,
            pltpu.SemaphoreType.DMA,
            pltpu.SemaphoreType.DMA((FWD_CHUNKS,)),
            pltpu.SemaphoreType.DMA,
            pltpu.SemaphoreType.DMA((INV_CHUNKS,)),
        ],
        compiler_params=pltpu.CompilerParams(
            collective_id=0, has_side_effects=True, vmem_limit_bytes=52 << 20
        ),
    )(tiles(limbs_a), tiles(limbs_b), jnp.asarray(matrix_tables()), jnp.asarray(vector_tables()))
    return out.reshape(4, 128, 8, 128).transpose(0, 2, 1, 3).reshape(LOCAL, ROWS)


def solution(mesh):
    placed = (P(("fft", "grp"), None), P(("fft", "grp"), None))
    return jax.shard_map(
        on_device, mesh=mesh, in_specs=placed, out_specs=P(("fft", "grp"), None), check_vma=False
    )
```

```python
import functools
import math

import jax
import jax.numpy as jnp
import ml_dtypes
import numpy as np
from jax import lax
from jax.experimental import pallas as pl
from jax.experimental.pallas import tpu as pltpu
from jax.sharding import PartitionSpec as P

MESH = pl.DeviceIdType.MESH
ROWS = 16384
COLS = 4096
TOTAL = ROWS * COLS
DIGIT_VAR = 5461.25
DEV = 128
LOCAL = COLS // DEV
HALVES = 2
PAIRS = LOCAL // 2
FWD_CHUNKS = 4
INV_CHUNKS = 2
F32 = jnp.float32
BF16 = jnp.bfloat16


def turn(num, den):
    angle = (np.asarray(num, np.int64) % den) * (2.0 * math.pi / den)
    return np.cos(angle), np.sin(angle)


def split_pair(table):
    high = table.astype(ml_dtypes.bfloat16)
    low = (table - high.astype(np.float64)).astype(ml_dtypes.bfloat16)
    return high, low


@functools.lru_cache(None)
def matrix_tables():
    ka = np.arange(128)
    lane = np.arange(64)
    order = np.concatenate([2 * np.arange(64), 2 * np.arange(64) + 1])
    c, s = turn(np.outer(2 * ka + 1, order), 512)
    first = split_pair(np.concatenate([c, -s], 0))
    first = np.concatenate([first[0], first[1]], 1)
    c, s = turn(np.outer(lane, lane), 64)
    z = np.zeros_like(c)
    c2, s2 = np.block([[c, z], [z, c]]), np.block([[s, z], [z, s]])
    lanes_inv = split_pair(np.block([[c2, s2], [-s2, c2]]))
    at = np.arange(128)
    at = at // 64 * 32 + at % 64 // 32 * 64 + at % 32
    c2, s2 = c2[:, at], s2[:, at]
    lanes_fwd = split_pair(np.block([[c2, -s2], [s2, c2]]))
    c, s = turn(np.outer(ka, ka), 128)
    dev_fwd = split_pair(np.block([[c, s], [-s, c]]))
    dev_inv = split_pair(np.block([[c, -s], [s, c]]))
    scale = 2.0 / (TOTAL * DIGIT_VAR * math.sqrt(TOTAL // 2))
    order = np.concatenate([2 * np.arange(128), 2 * np.arange(128) + 1])
    c, s = turn(np.outer(order, 2 * ka + 1), 512)
    last = split_pair(np.concatenate([c, -s], 1) * scale)
    mats = [first, *lanes_fwd, *dev_fwd, *dev_inv, *lanes_inv, *last]
    return np.stack(mats)


@functools.lru_cache(None)
def vector_tables():
    ka = np.arange(128)[:, None]
    lane = np.arange(128)[None, :]
    low, par = lane % 64, lane // 64
    two = par + 2 * (lane % 64 // 32)
    zero = 0 * lane
    k1 = ka + 256 * low
    k1_sent = ka + 256 * (32 * par + lane % 32)
    pairs = [
        turn(-low * (2 * ka + 1), 2 * ROWS),
        turn(-(2 * k1_sent + 1), 2 * TOTAL),
        turn(-ka * par, COLS),
        turn(-2 * ka + zero, COLS),
        turn(ka * two, COLS),
        turn(4 * ka + zero, COLS),
        turn(2 * (2 * k1 + 1), 2 * TOTAL),
        turn(par * (2 * k1 + 1), 2 * TOTAL),
        turn(-ka * par, 32),
        turn(ka * two, 32),
    ]
    return np.stack([t for pair in pairs for t in pair]).astype(np.float32)


def times(a, b):
    return a[0] * b[0] - a[1] * b[1], a[0] * b[1] + a[1] * b[0]


def turned(value, num, den):
    num %= den
    re, im = value
    if num == 0:
        return value
    if 4 * num == den:
        return -im, re
    if 2 * num == den:
        return -re, -im
    if 4 * num == 3 * den:
        return im, -re
    c, s = math.cos(2 * math.pi * num / den), math.sin(2 * math.pi * num / den)
    if 8 * num % den == 0:
        root = math.sqrt(0.5)
        sc, ss = math.copysign(1.0, c), math.copysign(1.0, s)
        first = re if sc > 0 else -re
        first = first - im if ss > 0 else first + im
        second = re if ss > 0 else -re
        second = second + im if sc > 0 else second - im
        return first * root, second * root
    return re * c - im * s, re * s + im * c


def small_dft(values, sign):
    n = len(values)
    if n == 1:
        return values
    half = n // 2
    even = [(a[0] + b[0], a[1] + b[1]) for a, b in zip(values[:half], values[half:])]
    odd = [
        turned((a[0] - b[0], a[1] - b[1]), sign * i, n)
        for i, (a, b) in enumerate(zip(values[:half], values[half:]))
    ]
    even, odd = small_dft(even, sign), small_dft(odd, sign)
    return [v for pair in zip(even, odd) for v in pair]


def halves(value):
    high = value.astype(BF16)
    return high, (value - high.astype(F32)).astype(BF16)


def dot(a, b):
    return jnp.dot(a, b, preferred_element_type=F32)


def kernel(
    a_hbm, b_hbm, mats_hbm, vecs_hbm, out_ref,
    a_ref, b_ref, mats, vecs, sent, got, mid, quot, back, home, turn_f, turn_d,
    in_sem, ready, send_f, recv_f, send_i, recv_i,
):
    fft, grp = lax.axis_index("fft"), lax.axis_index("grp")
    me = fft * 2 + grp
    barrier = pltpu.get_barrier_semaphore()

    loads = [
        pltpu.make_async_copy(src, dst, in_sem.at[i])
        for i, (src, dst) in enumerate(
            ((vecs_hbm, vecs), (a_hbm, a_ref), (b_hbm, b_ref), (mats_hbm, mats))
        )
    ]
    for load in loads:
        load.start()

    high, low = lax.div(me, 16), lax.rem(me, 16)

    def signal(sem, peer):
        pl.semaphore_signal(
            sem, inc=1, device_id=(lax.div(peer, 2), lax.rem(peer, 2)), device_id_type=MESH
        )

    for step in range(1, 16):
        signal(barrier, high * 16 + lax.rem(low + step, 16))
    across = [lax.rem(high + step, 8) * 16 + low for step in range(1, 8)]
    for peer in across:
        signal(barrier, peer)

    core, z, x = lax.rem(fft, 2), lax.rem(lax.div(fft, 2), 4), lax.rem(lax.div(fft, 8), 4)
    y = lax.div(fft, 32) * 2 + grp
    z_core = [
        lax.rem(z + j % 4, 4) * 2 + (core if j < 4 else 1 - core) for j in range(8)
    ]

    def each_peer(visit):
        def eight(dx, dy, first):
            xs = [lax.rem(x + (dx + t), 4) * 8 for t in range(4)]
            ys = [lax.rem(y + (dy + t), 4) for t in range(4)]
            highs = [lax.div(v, 2) * 32 for v in ys]
            lows = [lax.rem(v, 2) for v in ys]
            for j in range(first, 8):
                t = (2 * j + j // 2) % 4
                visit(z_core[j] + xs[(j + j // 4) % 4] + highs[t], lows[t])

        eight(0, 0, 1)

        def some(i, _):
            eight(lax.div(i, 4), lax.rem(i, 4), 0)
            return 0

        lax.fori_loop(1, 16, some, 0)

    def scatter(src, dst, first, count, send_sem, recv_sem):
        part = pl.ds(first, count)
        own = pl.ds(me, 1)
        pltpu.make_async_copy(src.at[part, :, own], dst.at[part, :, own], recv_sem).start()

        def send(peer_fft, peer_grp):
            pltpu.make_async_remote_copy(
                src_ref=src.at[part, :, pl.ds(peer_fft * 2 + peer_grp, 1)],
                dst_ref=dst.at[part, :, own],
                send_sem=send_sem,
                recv_sem=recv_sem,
                device_id=(peer_fft, peer_grp),
                device_id_type=MESH,
            ).start()

        each_peer(send)

    def arrived(src, dst, first, count, recv_sem):
        part = pl.ds(first, count)
        pltpu.make_async_copy(src.at[part], dst.at[part], recv_sem).wait()

    def all_sent(src, dst, send_sem):
        part = pl.ds(0, DEV - 1)
        pltpu.make_async_copy(src.at[:, :, part], dst.at[:, :, part], send_sem).wait()

    row = lax.broadcasted_iota(jnp.int32, (128, 128), 0)
    lane = lax.broadcasted_iota(jnp.int32, (128, 128), 1)
    left = lane < 64
    low32 = lax.rem(lane, 64) < 32
    tw = lambda i: (vecs[2 * i], vecs[2 * i + 1])

    def own_turn(kb):
        angle = (me * (2 * (row + 256 * kb) + 1)).astype(F32)
        angle = angle * (2.0 * math.pi / (2 * TOTAL // LOCAL))
        return jnp.cos(angle), jnp.sin(angle)

    c, s = own_turn(32 * lax.div(lane, 64) + lax.rem(lane, 32))
    turn_f[0], turn_f[1] = c, -s
    for load in loads:
        load.wait()
    pl.semaphore_wait(barrier, 22)
    for peer in across:
        signal(ready, peer)

    def forward(g, _):
        for pair in range(0, 8, 2):
            cols = []
            for cs in (pair, pair + 1):
                a = a_ref[g, pl.ds(cs, 64, stride=8), :].astype(F32)
                b = b_ref[g, pl.ds(cs, 64, stride=8), :].astype(F32)
                lo = jnp.where(left[:64], a, pltpu.roll(b, 64, 1))
                hi = jnp.where(left[:64], pltpu.roll(a, 64, 1), b)
                cols.append(jnp.concatenate([lo, hi], 0).astype(BF16))
            u_in = jnp.concatenate(cols, 1)
            u = dot(mats[0], jnp.concatenate([u_in, u_in], 0))
            rows = []
            for i in range(2):
                v = times((u[:128, 128 * i : 128 * i + 128], u[128:, 128 * i : 128 * i + 128]), tw(0))
                rows.append(jnp.concatenate(v, 1))
            vh, vl = halves(jnp.concatenate(rows, 0))
            f = dot(vh, mats[1]) + dot(vl, mats[1]) + dot(vh, mats[2])
            r = []
            for i in range(2):
                t = (turn_f[0], turn_f[1])
                r.append(times((f[128 * i : 128 * i + 128, :128], f[128 * i : 128 * i + 128, 128:]), t))
                turn_f[0], turn_f[1] = times(t, tw(1))
            at = 4 * g + pair // 2
            for i in range(2):
                sent[at, i] = jnp.where(left, r[0][i], pltpu.roll(r[1][i], 64, 1))
                sent[PAIRS + at, i] = jnp.where(left, pltpu.roll(r[0][i], 64, 1), r[1][i])

        @pl.when(g == 0)
        def _():
            pl.semaphore_wait(ready, 7)

        scatter(sent, got, 4 * g, 4, send_f, recv_f.at[g])
        return 0

    lax.fori_loop(0, 4, forward, 0)

    def second(g, _):
        scatter(sent, got, PAIRS + 4 * g, 4, send_f, recv_f.at[4 + g])
        return 0

    lax.fori_loop(0, 4, second, 0)

    lane8 = lax.broadcasted_iota(jnp.int32, (8, 128), 1)
    left8 = lane8 < 64
    low8 = lax.rem(lane8, 64) < 32
    sign1 = jnp.where(left8, 1.0, -1.0).astype(F32)
    sign2 = jnp.where(low8, 1.0, -1.0).astype(F32)

    def columns(h, _):
        turn_d[0], turn_d[1] = tw(2)

        def devices_digit(g, _):
            first = PAIRS * h + 4 * g
            arrived(sent, got, first, 4, recv_f.at[4 * h + g])
            x_in = jnp.concatenate([got[first + i].reshape(256, 128) for i in range(4)], 1)
            xh, xl = halves(x_in)
            f = dot(mats[3], xh) + dot(mats[3], xl) + dot(mats[4], xh)
            for i in range(4):
                t = (turn_d[0], turn_d[1])
                r = times((f[:128, 128 * i : 128 * i + 128], f[128:, 128 * i : 128 * i + 128]), t)
                mid[4 * g + i, 0] = r[0]
                mid[4 * g + i, 1] = r[1]
                turn_d[0], turn_d[1] = times(t, tw(3))
            return 0

        lax.fori_loop(0, 4, devices_digit, 0)

        def product(t, _):
            rows = pl.ds(pl.multiple_of(8 * t, 8), 8)
            bins = small_dft([(mid[i, 0, rows, :], mid[i, 1, rows, :]) for i in range(PAIRS)], -1)
            folded = []
            for i, v in enumerate(bins):
                w = (vecs[16, pl.ds(i, 1), :], vecs[17, pl.ds(i, 1), :])
                v = times(v, w)
                v = tuple(pltpu.roll(e, 64, 1) + sign1 * e for e in v)
                o = tuple(jnp.where(low8, pltpu.roll(e, 96, 1), pltpu.roll(e, 32, 1)) for e in v)
                p = times(v, o)
                folded.append(tuple(pltpu.roll(e, 64, 1) + sign1 * e for e in p))
            packed = []
            for i in range(8):
                p, q = folded[i], folded[i + 8]
                q = (jnp.where(left8, q[0], -q[1]), jnp.where(left8, q[1], q[0]))
                w = (vecs[18, pl.ds(i, 1), :], vecs[19, pl.ds(i, 1), :])
                packed.append(times((p[0] + sign2 * q[0], p[1] + sign2 * q[1]), w))
            for i, v in enumerate(small_dft(packed, 1)):
                quot[i, 0, rows, :] = v[0]
                quot[i, 1, rows, :] = v[1]
            return 0

        lax.fori_loop(0, 16, product, 0)

        turn_d[0], turn_d[1] = tw(4)

        def devices_back(g, _):
            cols = []
            for i in range(4):
                t = (turn_d[0], turn_d[1])
                r = times((quot[4 * g + i, 0], quot[4 * g + i, 1]), t)
                cols.append(jnp.concatenate(r, 0))
                turn_d[0], turn_d[1] = times(t, tw(5))
            xh, xl = halves(jnp.concatenate(cols, 1))
            f = dot(mats[5], xh) + dot(mats[5], xl) + dot(mats[6], xh)
            first = 8 * h + 4 * g
            for i in range(4):
                back[first + i, 0] = f[:128, 128 * i : 128 * i + 128]
                back[first + i, 1] = f[128:, 128 * i : 128 * i + 128]
            scatter(back, home, first, 4, send_i, recv_i.at[2 * h + g])
            return 0

        lax.fori_loop(0, 2, devices_back, 0)
        return 0

    lax.fori_loop(0, HALVES, columns, 0)

    turn_f[0], turn_f[1] = times(own_turn(lax.rem(lane, 64)), tw(7))

    def inverse(g, _):
        @pl.when(lax.rem(g, 2) == 0)
        def _():
            arrived(back, home, 2 * g, 4, recv_i.at[lax.div(g, 2)])
            arrived(back, home, 8 + 2 * g, 4, recv_i.at[2 + lax.div(g, 2)])

        for pair in range(2):
            at = 2 * g + pair
            both = ([], [])
            for i in range(2):
                p, q = home[at, i], home[8 + at, i]
                both[0].append(jnp.where(low32, p, pltpu.roll(q, 32, 1)))
                both[1].append(jnp.where(low32, pltpu.roll(p, 96, 1), q))
            rows = []
            for v in both:
                t = (turn_f[0], turn_f[1])
                rows.append(jnp.concatenate(times(v, t), 1))
                turn_f[0], turn_f[1] = times(t, tw(6))
            xh, xl = halves(jnp.concatenate(rows, 0))
            v = dot(xh, mats[7]) + dot(xl, mats[7]) + dot(xh, mats[8])
            c, s = tw(0)
            cols = []
            for i in range(2):
                vi = times((v[128 * i : 128 * i + 128, :128], v[128 * i : 128 * i + 128, 128:]), (c, -s))
                cols.append(jnp.concatenate(vi, 0))
            vh, vl = halves(jnp.concatenate(cols, 1))
            o = dot(mats[9], vh) + dot(mats[9], vl) + dot(mats[10], vh)
            for i in range(2):
                o0, o1 = o[:128, 128 * i : 128 * i + 128], o[128:, 128 * i : 128 * i + 128]
                cs = 4 * pair + 2 * i
                out_ref[g, pl.ds(cs, 128, stride=8), :] = jnp.where(left, o0, pltpu.roll(o1, 64, 1))
                out_ref[g, pl.ds(cs + 1, 128, stride=8), :] = jnp.where(left, pltpu.roll(o0, 64, 1), o1)
        return 0

    lax.fori_loop(0, 4, inverse, 0)
    all_sent(sent, got, send_f)
    all_sent(back, home, send_i)


def on_device(limbs_a, limbs_b):
    def tiles(x):
        return x.reshape(4, 8, 64, 128).transpose(0, 2, 1, 3).reshape(4, 512, 128)

    out = pl.pallas_call(
        kernel,
        out_shape=pltpu.VMEM((4, 1024, 128), F32),
        in_specs=[pl.BlockSpec(memory_space=pltpu.HBM)] * 4,
        out_specs=pl.BlockSpec(memory_space=pltpu.VMEM),
        scratch_shapes=[
            pltpu.VMEM((4, 512, 128), jnp.int32),
            pltpu.VMEM((4, 512, 128), jnp.int32),
            pltpu.VMEM((11, 256, 256), BF16),
            pltpu.VMEM((20, 128, 128), F32),
            pltpu.VMEM((LOCAL, 2, 128, 128), F32),
            pltpu.VMEM((LOCAL, 2, 128, 128), F32),
            pltpu.VMEM((PAIRS, 2, 128, 128), F32),
            pltpu.VMEM((8, 2, 128, 128), F32),
            pltpu.VMEM((16, 2, 128, 128), F32),
            pltpu.VMEM((16, 2, 128, 128), F32),
            pltpu.VMEM((2, 128, 128), F32),
            pltpu.VMEM((2, 128, 128), F32),
            pltpu.SemaphoreType.DMA((4,)),
            pltpu.SemaphoreType.REGULAR,
            pltpu.SemaphoreType.DMA,
            pltpu.SemaphoreType.DMA((8,)),
            pltpu.SemaphoreType.DMA,
            pltpu.SemaphoreType.DMA((4,)),
        ],
        compiler_params=pltpu.CompilerParams(
            collective_id=0, has_side_effects=True, vmem_limit_bytes=60 << 20
        ),
    )(tiles(limbs_a), tiles(limbs_b), jnp.asarray(matrix_tables()), jnp.asarray(vector_tables()))
    return out.reshape(4, 128, 8, 128).transpose(0, 2, 1, 3).reshape(LOCAL, ROWS)


def solution(mesh):
    placed = (P(("fft", "grp"), None), P(("fft", "grp"), None))
    return jax.shard_map(
        on_device, mesh=mesh, in_specs=placed, out_specs=P(("fft", "grp"), None), check_vma=False
    )
```

```python
import functools
import math

import jax
import jax.numpy as jnp
import ml_dtypes
import numpy as np
from jax import lax
from jax.experimental import pallas as pl
from jax.experimental.pallas import tpu as pltpu
from jax.sharding import PartitionSpec as P

MESH = pl.DeviceIdType.MESH
ROWS = 16384
COLS = 4096
TOTAL = ROWS * COLS
DIGIT_VAR = 5461.25
DEV = 128
LOCAL = COLS // DEV
HALVES = 2
PAIRS = LOCAL // 2
FWD_CHUNKS = 4
INV_CHUNKS = 2
F32 = jnp.float32
BF16 = jnp.bfloat16


def turn(num, den):
    angle = (np.asarray(num, np.int64) % den) * (2.0 * math.pi / den)
    return np.cos(angle), np.sin(angle)


def split_pair(table):
    high = table.astype(ml_dtypes.bfloat16)
    low = (table - high.astype(np.float64)).astype(ml_dtypes.bfloat16)
    return high, low


@functools.lru_cache(None)
def matrix_tables():
    ka = np.arange(128)
    lane = np.arange(64)
    order = np.concatenate([2 * np.arange(64), 2 * np.arange(64) + 1])
    c, s = turn(np.outer(2 * ka + 1, order), 512)
    first = split_pair(np.concatenate([c, -s], 0))
    first = np.concatenate([first[0], first[1]], 1)
    c, s = turn(np.outer(lane, lane), 64)
    z = np.zeros_like(c)
    c2, s2 = np.block([[c, z], [z, c]]), np.block([[s, z], [z, s]])
    lanes_inv = split_pair(np.block([[c2, s2], [-s2, c2]]))
    at = np.arange(128)
    at = at // 64 * 32 + at % 64 // 32 * 64 + at % 32
    c2, s2 = c2[:, at], s2[:, at]
    lanes_fwd = split_pair(np.block([[c2, -s2], [s2, c2]]))
    c, s = turn(np.outer(ka, ka), 128)
    dev_fwd = split_pair(np.block([[c, s], [-s, c]]))
    dev_inv = split_pair(np.block([[c, -s], [s, c]]))
    scale = 2.0 / (TOTAL * DIGIT_VAR * math.sqrt(TOTAL // 2))
    order = np.concatenate([2 * np.arange(128), 2 * np.arange(128) + 1])
    c, s = turn(np.outer(order, 2 * ka + 1), 512)
    last = split_pair(np.concatenate([c, -s], 1) * scale)
    mats = [first, *lanes_fwd, *dev_fwd, *dev_inv, *lanes_inv, *last]
    return np.stack(mats)


@functools.lru_cache(None)
def vector_tables():
    ka = np.arange(128)[:, None]
    lane = np.arange(128)[None, :]
    low, par = lane % 64, lane // 64
    two = par + 2 * (lane % 64 // 32)
    zero = 0 * lane
    k1 = ka + 256 * low
    k1_sent = ka + 256 * (32 * par + lane % 32)
    pairs = [
        turn(-low * (2 * ka + 1), 2 * ROWS),
        turn(-(2 * k1_sent + 1), 2 * TOTAL),
        turn(-ka * par, COLS),
        turn(-2 * ka + zero, COLS),
        turn(ka * two, COLS),
        turn(4 * ka + zero, COLS),
        turn(2 * (2 * k1 + 1), 2 * TOTAL),
        turn(par * (2 * k1 + 1), 2 * TOTAL),
        turn(-ka * par, 32),
        turn(ka * two, 32),
    ]
    return np.stack([t for pair in pairs for t in pair]).astype(np.float32)


def times(a, b):
    return a[0] * b[0] - a[1] * b[1], a[0] * b[1] + a[1] * b[0]


def turned(value, num, den):
    num %= den
    re, im = value
    if num == 0:
        return value
    if 4 * num == den:
        return -im, re
    if 2 * num == den:
        return -re, -im
    if 4 * num == 3 * den:
        return im, -re
    c, s = math.cos(2 * math.pi * num / den), math.sin(2 * math.pi * num / den)
    if 8 * num % den == 0:
        root = math.sqrt(0.5)
        sc, ss = math.copysign(1.0, c), math.copysign(1.0, s)
        first = re if sc > 0 else -re
        first = first - im if ss > 0 else first + im
        second = re if ss > 0 else -re
        second = second + im if sc > 0 else second - im
        return first * root, second * root
    return re * c - im * s, re * s + im * c


def small_dft(values, sign):
    n = len(values)
    if n == 1:
        return values
    half = n // 2
    even = [(a[0] + b[0], a[1] + b[1]) for a, b in zip(values[:half], values[half:])]
    odd = [
        turned((a[0] - b[0], a[1] - b[1]), sign * i, n)
        for i, (a, b) in enumerate(zip(values[:half], values[half:]))
    ]
    even, odd = small_dft(even, sign), small_dft(odd, sign)
    return [v for pair in zip(even, odd) for v in pair]


def halves(value):
    high = value.astype(BF16)
    return high, (value - high.astype(F32)).astype(BF16)


def dot(a, b):
    return jnp.dot(a, b, preferred_element_type=F32)


def kernel(
    a_hbm, b_hbm, mats_hbm, vecs_hbm, out_ref,
    a_ref, b_ref, mats, vecs, sent, got, mid, quot, back, home, turn_f, turn_d,
    in_sem, ready, send_f, recv_f, send_i, recv_i,
):
    fft, grp = lax.axis_index("fft"), lax.axis_index("grp")
    me = fft * 2 + grp
    barrier = pltpu.get_barrier_semaphore()

    parts = [(a_hbm, a_ref, 0, 1), (b_hbm, b_ref, 0, 1), (mats_hbm, mats, 0, 3), (vecs_hbm, vecs, 0, 4)]
    parts += [(a_hbm, a_ref, 1, 3), (b_hbm, b_ref, 1, 3), (mats_hbm, mats, 3, 8), (vecs_hbm, vecs, 4, 16)]
    loads = [
        pltpu.make_async_copy(src.at[pl.ds(at, n)], dst.at[pl.ds(at, n)], in_sem.at[i])
        for i, (src, dst, at, n) in enumerate(parts)
    ]
    for load in loads:
        load.start()

    high, low = lax.div(me, 16), lax.rem(me, 16)

    def signal(sem, peer):
        pl.semaphore_signal(
            sem, inc=1, device_id=(lax.div(peer, 2), lax.rem(peer, 2)), device_id_type=MESH
        )

    for step in range(1, 16):
        signal(barrier, high * 16 + lax.rem(low + step, 16))
    across = [lax.rem(high + step, 8) * 16 + low for step in range(1, 8)]
    for peer in across:
        signal(barrier, peer)

    core, z, x = lax.rem(fft, 2), lax.rem(lax.div(fft, 2), 4), lax.rem(lax.div(fft, 8), 4)
    y = lax.div(fft, 32) * 2 + grp
    z_core = [
        lax.rem(z + j % 4, 4) * 2 + (core if j < 4 else 1 - core) for j in range(8)
    ]

    def each_peer(visit):
        def eight(dx, dy, first):
            xs = [lax.rem(x + (dx + t), 4) * 8 for t in range(4)]
            ys = [lax.rem(y + (dy + t), 4) for t in range(4)]
            highs = [lax.div(v, 2) * 32 for v in ys]
            lows = [lax.rem(v, 2) for v in ys]
            for j in range(first, 8):
                t = (2 * j + j // 2) % 4
                visit(z_core[j] + xs[(j + j // 4) % 4] + highs[t], lows[t])

        eight(0, 0, 1)

        def some(i, _):
            eight(lax.div(i, 4), lax.rem(i, 4), 0)
            return 0

        lax.fori_loop(1, 16, some, 0)

    def scatter(src, dst, first, count, send_sem, recv_sem):
        part = pl.ds(first, count)
        own = pl.ds(me, 1)
        pltpu.make_async_copy(src.at[part, :, own], dst.at[part, :, own], recv_sem).start()

        def send(peer_fft, peer_grp):
            pltpu.make_async_remote_copy(
                src_ref=src.at[part, :, pl.ds(peer_fft * 2 + peer_grp, 1)],
                dst_ref=dst.at[part, :, own],
                send_sem=send_sem,
                recv_sem=recv_sem,
                device_id=(peer_fft, peer_grp),
                device_id_type=MESH,
            ).start()

        each_peer(send)

    def arrived(src, dst, first, count, recv_sem):
        part = pl.ds(first, count)
        pltpu.make_async_copy(src.at[part], dst.at[part], recv_sem).wait()

    def all_sent(src, dst, send_sem):
        part = pl.ds(0, DEV - 1)
        pltpu.make_async_copy(src.at[:, :, part], dst.at[:, :, part], send_sem).wait()

    row = lax.broadcasted_iota(jnp.int32, (128, 128), 0)
    lane = lax.broadcasted_iota(jnp.int32, (128, 128), 1)
    left = lane < 64
    low32 = lax.rem(lane, 64) < 32
    tw = lambda i: (vecs[2 * i], vecs[2 * i + 1])

    def own_turn(kb):
        angle = (me * (2 * (row + 256 * kb) + 1)).astype(F32)
        angle = angle * (2.0 * math.pi / (2 * TOTAL // LOCAL))
        return jnp.cos(angle), jnp.sin(angle)

    c, s = own_turn(32 * lax.div(lane, 64) + lax.rem(lane, 32))
    turn_f[0], turn_f[1] = c, -s
    for load in loads[:4]:
        load.wait()

    def rows_forward(g, first, last):
        for pair in range(first, last, 2):
            cols = []
            for cs in (pair, pair + 1):
                a = a_ref[g, pl.ds(cs, 64, stride=8), :].astype(F32)
                b = b_ref[g, pl.ds(cs, 64, stride=8), :].astype(F32)
                lo = jnp.where(left[:64], a, pltpu.roll(b, 64, 1))
                hi = jnp.where(left[:64], pltpu.roll(a, 64, 1), b)
                cols.append(jnp.concatenate([lo, hi], 0).astype(BF16))
            u_in = jnp.concatenate(cols, 1)
            u = dot(mats[0], jnp.concatenate([u_in, u_in], 0))
            rows = []
            for i in range(2):
                v = times((u[:128, 128 * i : 128 * i + 128], u[128:, 128 * i : 128 * i + 128]), tw(0))
                rows.append(jnp.concatenate(v, 1))
            vh, vl = halves(jnp.concatenate(rows, 0))
            f = dot(vh, mats[1]) + dot(vl, mats[1]) + dot(vh, mats[2])
            r = []
            for i in range(2):
                t = (turn_f[0], turn_f[1])
                r.append(times((f[128 * i : 128 * i + 128, :128], f[128 * i : 128 * i + 128, 128:]), t))
                turn_f[0], turn_f[1] = times(t, tw(1))
            at = 4 * g + pair // 2
            for i in range(2):
                sent[at, i] = jnp.where(left, r[0][i], pltpu.roll(r[1][i], 64, 1))
                sent[PAIRS + at, i] = jnp.where(left, pltpu.roll(r[0][i], 64, 1), r[1][i])

    def forward(g, _):
        rows_forward(g, 0, 8)
        scatter(sent, got, 4 * g, 4, send_f, recv_f.at[g])
        return 0

    rows_forward(0, 0, 4)
    pl.semaphore_wait(barrier, 22)
    for step, peer in enumerate(across):
        signal(ready.at[step], peer)
    first_part, own = pl.ds(0, 2), pl.ds(me, 1)
    pltpu.make_async_copy(sent.at[first_part, :, own], got.at[first_part, :, own], recv_f.at[8]).start()

    def first_send(peer):
        pltpu.make_async_remote_copy(
            src_ref=sent.at[first_part, :, pl.ds(peer, 1)],
            dst_ref=got.at[first_part, :, own],
            send_sem=send_f,
            recv_sem=recv_f.at[8],
            device_id=(lax.div(peer, 2), lax.rem(peer, 2)),
            device_id_type=MESH,
        ).start()

    for step in range(1, 16):
        first_send(high * 16 + lax.rem(low + step, 16))

    def first_sends(step, _):
        pl.semaphore_wait(ready.at[step - 1], 1)
        base = lax.rem(high + 8 - step, 8) * 16

        def some(i, _):
            for j in range(4):
                first_send(base + lax.rem(low + 4 * i + j, 16))
            return 0

        lax.fori_loop(0, 4, some, 0)
        return 0

    lax.fori_loop(1, 8, first_sends, 0)
    for load in loads[4:]:
        load.wait()
    rows_forward(0, 4, 8)
    scatter(sent, got, 2, 2, send_f, recv_f.at[0])
    lax.fori_loop(1, 4, forward, 0)

    def second(g, _):
        scatter(sent, got, PAIRS + 4 * g, 4, send_f, recv_f.at[4 + g])
        return 0

    lax.fori_loop(0, 4, second, 0)

    lane8 = lax.broadcasted_iota(jnp.int32, (8, 128), 1)
    left8 = lane8 < 64
    low8 = lax.rem(lane8, 64) < 32
    sign1 = jnp.where(left8, 1.0, -1.0).astype(F32)
    sign2 = jnp.where(low8, 1.0, -1.0).astype(F32)

    def columns(h, _):
        turn_d[0], turn_d[1] = tw(2)

        def devices_digit(g, _):
            first = PAIRS * h + 4 * g
            start = jnp.logical_and(h == 0, g == 0)

            @pl.when(start)
            def _():
                arrived(sent, got, 0, 2, recv_f.at[8])
                arrived(sent, got, 2, 2, recv_f.at[0])

            @pl.when(jnp.logical_not(start))
            def _():
                arrived(sent, got, first, 4, recv_f.at[4 * h + g])

            x_in = jnp.concatenate([got[first + i].reshape(256, 128) for i in range(4)], 1)
            xh, xl = halves(x_in)
            f = dot(mats[3], xh) + dot(mats[3], xl) + dot(mats[4], xh)
            for i in range(4):
                t = (turn_d[0], turn_d[1])
                r = times((f[:128, 128 * i : 128 * i + 128], f[128:, 128 * i : 128 * i + 128]), t)
                mid[4 * g + i, 0] = r[0]
                mid[4 * g + i, 1] = r[1]
                turn_d[0], turn_d[1] = times(t, tw(3))
            return 0

        lax.fori_loop(0, 4, devices_digit, 0)

        def product(t, _):
            rows = pl.ds(pl.multiple_of(8 * t, 8), 8)
            bins = small_dft([(mid[i, 0, rows, :], mid[i, 1, rows, :]) for i in range(PAIRS)], -1)
            folded = []
            for i, v in enumerate(bins):
                w = (vecs[16, pl.ds(i, 1), :], vecs[17, pl.ds(i, 1), :])
                v = times(v, w)
                v = tuple(pltpu.roll(e, 64, 1) + sign1 * e for e in v)
                o = tuple(jnp.where(low8, pltpu.roll(e, 96, 1), pltpu.roll(e, 32, 1)) for e in v)
                p = times(v, o)
                folded.append(tuple(pltpu.roll(e, 64, 1) + sign1 * e for e in p))
            packed = []
            for i in range(8):
                p, q = folded[i], folded[i + 8]
                q = (jnp.where(left8, q[0], -q[1]), jnp.where(left8, q[1], q[0]))
                w = (vecs[18, pl.ds(i, 1), :], vecs[19, pl.ds(i, 1), :])
                packed.append(times((p[0] + sign2 * q[0], p[1] + sign2 * q[1]), w))
            for i, v in enumerate(small_dft(packed, 1)):
                quot[i, 0, rows, :] = v[0]
                quot[i, 1, rows, :] = v[1]
            return 0

        lax.fori_loop(0, 16, product, 0)

        turn_d[0], turn_d[1] = tw(4)

        def devices_back(g, _):
            cols = []
            for i in range(4):
                t = (turn_d[0], turn_d[1])
                r = times((quot[4 * g + i, 0], quot[4 * g + i, 1]), t)
                cols.append(jnp.concatenate(r, 0))
                turn_d[0], turn_d[1] = times(t, tw(5))
            xh, xl = halves(jnp.concatenate(cols, 1))
            f = dot(mats[5], xh) + dot(mats[5], xl) + dot(mats[6], xh)
            first = 8 * h + 4 * g
            for i in range(4):
                back[first + i, 0] = f[:128, 128 * i : 128 * i + 128]
                back[first + i, 1] = f[128:, 128 * i : 128 * i + 128]
            scatter(back, home, first, 2, send_i, recv_i.at[4 * h + 2 * g])
            scatter(back, home, first + 2, 2, send_i, recv_i.at[4 * h + 2 * g + 1])
            return 0

        lax.fori_loop(0, 2, devices_back, 0)
        return 0

    lax.fori_loop(0, HALVES, columns, 0)

    turn_f[0], turn_f[1] = times(own_turn(lax.rem(lane, 64)), tw(7))

    def inverse(g, _):
        arrived(back, home, 2 * g, 2, recv_i.at[g])
        arrived(back, home, 8 + 2 * g, 2, recv_i.at[4 + g])

        for pair in range(2):
            at = 2 * g + pair
            both = ([], [])
            for i in range(2):
                p, q = home[at, i], home[8 + at, i]
                both[0].append(jnp.where(low32, p, pltpu.roll(q, 32, 1)))
                both[1].append(jnp.where(low32, pltpu.roll(p, 96, 1), q))
            rows = []
            for v in both:
                t = (turn_f[0], turn_f[1])
                rows.append(jnp.concatenate(times(v, t), 1))
                turn_f[0], turn_f[1] = times(t, tw(6))
            xh, xl = halves(jnp.concatenate(rows, 0))
            v = dot(xh, mats[7]) + dot(xl, mats[7]) + dot(xh, mats[8])
            c, s = tw(0)
            cols = []
            for i in range(2):
                vi = times((v[128 * i : 128 * i + 128, :128], v[128 * i : 128 * i + 128, 128:]), (c, -s))
                cols.append(jnp.concatenate(vi, 0))
            vh, vl = halves(jnp.concatenate(cols, 1))
            o = dot(mats[9], vh) + dot(mats[9], vl) + dot(mats[10], vh)
            for i in range(2):
                o0, o1 = o[:128, 128 * i : 128 * i + 128], o[128:, 128 * i : 128 * i + 128]
                cs = 4 * pair + 2 * i
                out_ref[g, pl.ds(cs, 128, stride=8), :] = jnp.where(left, o0, pltpu.roll(o1, 64, 1))
                out_ref[g, pl.ds(cs + 1, 128, stride=8), :] = jnp.where(left, pltpu.roll(o0, 64, 1), o1)
        return 0

    lax.fori_loop(0, 4, inverse, 0)
    all_sent(sent, got, send_f)
    all_sent(back, home, send_i)


def on_device(limbs_a, limbs_b):
    def tiles(x):
        return x.reshape(4, 8, 64, 128).transpose(0, 2, 1, 3).reshape(4, 512, 128)

    out = pl.pallas_call(
        kernel,
        out_shape=pltpu.VMEM((4, 1024, 128), F32),
        in_specs=[pl.BlockSpec(memory_space=pltpu.HBM)] * 4,
        out_specs=pl.BlockSpec(memory_space=pltpu.VMEM),
        scratch_shapes=[
            pltpu.VMEM((4, 512, 128), jnp.int32),
            pltpu.VMEM((4, 512, 128), jnp.int32),
            pltpu.VMEM((11, 256, 256), BF16),
            pltpu.VMEM((20, 128, 128), F32),
            pltpu.VMEM((LOCAL, 2, 128, 128), F32),
            pltpu.VMEM((LOCAL, 2, 128, 128), F32),
            pltpu.VMEM((PAIRS, 2, 128, 128), F32),
            pltpu.VMEM((8, 2, 128, 128), F32),
            pltpu.VMEM((16, 2, 128, 128), F32),
            pltpu.VMEM((16, 2, 128, 128), F32),
            pltpu.VMEM((2, 128, 128), F32),
            pltpu.VMEM((2, 128, 128), F32),
            pltpu.SemaphoreType.DMA((8,)),
            pltpu.SemaphoreType.REGULAR((7,)),
            pltpu.SemaphoreType.DMA,
            pltpu.SemaphoreType.DMA((9,)),
            pltpu.SemaphoreType.DMA,
            pltpu.SemaphoreType.DMA((8,)),
        ],
        compiler_params=pltpu.CompilerParams(
            collective_id=0, has_side_effects=True, vmem_limit_bytes=60 << 20
        ),
    )(tiles(limbs_a), tiles(limbs_b), jnp.asarray(matrix_tables()), jnp.asarray(vector_tables()))
    return out.reshape(4, 128, 8, 128).transpose(0, 2, 1, 3).reshape(LOCAL, ROWS)


def solution(mesh):
    placed = (P(("fft", "grp"), None), P(("fft", "grp"), None))
    return jax.shard_map(
        on_device, mesh=mesh, in_specs=placed, out_specs=P(("fft", "grp"), None), check_vma=False
    )
```

```python
import functools
import math

import jax
import jax.numpy as jnp
import ml_dtypes
import numpy as np
from jax import lax
from jax.experimental import pallas as pl
from jax.experimental.pallas import tpu as pltpu
from jax.sharding import PartitionSpec as P

MESH = pl.DeviceIdType.MESH
ROWS = 16384
COLS = 4096
TOTAL = ROWS * COLS
DIGIT_VAR = 5461.25
DEV = 128
LOCAL = COLS // DEV
HALVES = 2
PAIRS = LOCAL // 2
FWD_CHUNKS = 4
INV_CHUNKS = 2
F32 = jnp.float32
BF16 = jnp.bfloat16


def turn(num, den):
    angle = (np.asarray(num, np.int64) % den) * (2.0 * math.pi / den)
    return np.cos(angle), np.sin(angle)


def split_pair(table):
    high = table.astype(ml_dtypes.bfloat16)
    low = (table - high.astype(np.float64)).astype(ml_dtypes.bfloat16)
    return high, low


@functools.lru_cache(None)
def matrix_tables():
    ka = np.arange(128)
    lane = np.arange(64)
    order = np.concatenate([2 * np.arange(64), 2 * np.arange(64) + 1])
    c, s = turn(np.outer(2 * ka + 1, order), 512)
    first = split_pair(np.concatenate([c, -s], 0))
    first = np.concatenate([first[0], first[1]], 1)
    c, s = turn(np.outer(lane, lane), 64)
    z = np.zeros_like(c)
    c2, s2 = np.block([[c, z], [z, c]]), np.block([[s, z], [z, s]])
    lanes_inv = split_pair(np.block([[c2, s2], [-s2, c2]]))
    at = np.arange(128)
    at = at // 64 * 32 + at % 64 // 32 * 64 + at % 32
    c2, s2 = c2[:, at], s2[:, at]
    lanes_fwd = split_pair(np.block([[c2, -s2], [s2, c2]]))
    c, s = turn(np.outer(ka, ka), 128)
    dev_fwd = split_pair(np.block([[c, s], [-s, c]]))
    dev_inv = split_pair(np.block([[c, -s], [s, c]]))
    scale = 2.0 / (TOTAL * DIGIT_VAR * math.sqrt(TOTAL // 2))
    order = np.concatenate([2 * np.arange(128), 2 * np.arange(128) + 1])
    c, s = turn(np.outer(order, 2 * ka + 1), 512)
    last = split_pair(np.concatenate([c, -s], 1) * scale)
    mats = [first, *lanes_fwd, *dev_fwd, *dev_inv, *lanes_inv, *last]
    return np.stack(mats)


@functools.lru_cache(None)
def vector_tables():
    ka = np.arange(128)[:, None]
    lane = np.arange(128)[None, :]
    low, par = lane % 64, lane // 64
    two = par + 2 * (lane % 64 // 32)
    zero = 0 * lane
    k1 = ka + 256 * low
    k1_sent = ka + 256 * (32 * par + lane % 32)
    pairs = [
        turn(-low * (2 * ka + 1), 2 * ROWS),
        turn(-(2 * k1_sent + 1), 2 * TOTAL),
        turn(-ka * par, COLS),
        turn(-2 * ka + zero, COLS),
        turn(ka * two, COLS),
        turn(4 * ka + zero, COLS),
        turn(2 * (2 * k1 + 1), 2 * TOTAL),
        turn(par * (2 * k1 + 1), 2 * TOTAL),
        turn(-ka * par, 32),
        turn(ka * two, 32),
    ]
    return np.stack([t for pair in pairs for t in pair]).astype(np.float32)


def all_displacements():
    out = []
    for i in range(16):
        for j in range(8):
            dx, dy = i // 4 + j + j // 4, i % 4 + 2 * j + j // 2
            out.append((dx % 4, dy % 4, j % 4, j // 4))
    return out[1:]


PEERS = all_displacements()


def hops(place):
    return sum(min(v, 4 - v) for v in place[:3])


def times(a, b):
    return a[0] * b[0] - a[1] * b[1], a[0] * b[1] + a[1] * b[0]


def turned(value, num, den):
    num %= den
    re, im = value
    if num == 0:
        return value
    if 4 * num == den:
        return -im, re
    if 2 * num == den:
        return -re, -im
    if 4 * num == 3 * den:
        return im, -re
    c, s = math.cos(2 * math.pi * num / den), math.sin(2 * math.pi * num / den)
    if 8 * num % den == 0:
        root = math.sqrt(0.5)
        sc, ss = math.copysign(1.0, c), math.copysign(1.0, s)
        first = re if sc > 0 else -re
        first = first - im if ss > 0 else first + im
        second = re if ss > 0 else -re
        second = second + im if sc > 0 else second - im
        return first * root, second * root
    return re * c - im * s, re * s + im * c


def small_dft(values, sign):
    n = len(values)
    if n == 1:
        return values
    half = n // 2
    even = [(a[0] + b[0], a[1] + b[1]) for a, b in zip(values[:half], values[half:])]
    odd = [
        turned((a[0] - b[0], a[1] - b[1]), sign * i, n)
        for i, (a, b) in enumerate(zip(values[:half], values[half:]))
    ]
    even, odd = small_dft(even, sign), small_dft(odd, sign)
    return [v for pair in zip(even, odd) for v in pair]


def halves(value):
    high = value.astype(BF16)
    return high, (value - high.astype(F32)).astype(BF16)


def dot(a, b):
    return jnp.dot(a, b, preferred_element_type=F32)


def kernel(
    a_hbm, b_hbm, mats_hbm, vecs_hbm, out_ref,
    a_ref, b_ref, mats, vecs, sent, got, mid, quot, back, home, turn_f, turn_d,
    in_sem, send_f, recv_f, send_i, recv_i,
):
    fft, grp = lax.axis_index("fft"), lax.axis_index("grp")
    me = fft * 2 + grp
    barrier = pltpu.get_barrier_semaphore()

    parts = [(a_hbm, a_ref, 0, 1), (b_hbm, b_ref, 0, 1), (mats_hbm, mats, 0, 3), (vecs_hbm, vecs, 0, 4)]
    parts += [(a_hbm, a_ref, 1, 3), (b_hbm, b_ref, 1, 3), (mats_hbm, mats, 3, 8), (vecs_hbm, vecs, 4, 16)]
    loads = [
        pltpu.make_async_copy(src.at[pl.ds(at, n)], dst.at[pl.ds(at, n)], in_sem.at[i])
        for i, (src, dst, at, n) in enumerate(parts)
    ]
    for load in loads:
        load.start()

    core, z, x = lax.rem(fft, 2), lax.rem(lax.div(fft, 2), 4), lax.rem(lax.div(fft, 8), 4)
    y = lax.div(fft, 32) * 2 + grp
    cores = [core, 1 - core]
    zs = [lax.rem(z + t, 4) * 2 for t in range(4)]
    xs = [lax.rem(x + t, 4) * 8 for t in range(4)]
    ys = [lax.rem(y + t, 4) for t in range(4)]
    highs = [lax.div(v, 2) * 32 for v in ys]
    lows = [lax.rem(v, 2) for v in ys]

    def peer_at(dx, dy, dz, dc):
        return highs[dy] + xs[dx] + zs[dz] + cores[dc], lows[dy]

    def signal(sem, place):
        pl.semaphore_signal(sem, inc=1, device_id=peer_at(*place), device_id_type=MESH)

    for place in sorted(PEERS, key=lambda d: -hops(d)):
        signal(barrier, place)

    def send(src, dst, part, place, send_sem, recv_sem):
        peer = peer_at(*place)
        pltpu.make_async_remote_copy(
            src_ref=src.at[part, :, pl.ds(peer[0] * 2 + peer[1], 1)],
            dst_ref=dst.at[part, :, pl.ds(me, 1)],
            send_sem=send_sem,
            recv_sem=recv_sem,
            device_id=peer,
            device_id_type=MESH,
        ).start()

    def scatter(src, dst, first, count, send_sem, recv_sem):
        part = pl.ds(first, count)
        own = pl.ds(me, 1)
        pltpu.make_async_copy(src.at[part, :, own], dst.at[part, :, own], recv_sem).start()

        for place in PEERS:
            send(src, dst, part, place, send_sem, recv_sem)

    def arrived(src, dst, first, count, recv_sem):
        part = pl.ds(first, count)
        pltpu.make_async_copy(src.at[part], dst.at[part], recv_sem).wait()

    def all_sent(src, dst, send_sem):
        part = pl.ds(0, DEV - 1)
        pltpu.make_async_copy(src.at[:, :, part], dst.at[:, :, part], send_sem).wait()

    row = lax.broadcasted_iota(jnp.int32, (128, 128), 0)
    lane = lax.broadcasted_iota(jnp.int32, (128, 128), 1)
    left = lane < 64
    low32 = lax.rem(lane, 64) < 32
    tw = lambda i: (vecs[2 * i], vecs[2 * i + 1])

    def own_turn(kb):
        angle = (me * (2 * (row + 256 * kb) + 1)).astype(F32)
        angle = angle * (2.0 * math.pi / (2 * TOTAL // LOCAL))
        return jnp.cos(angle), jnp.sin(angle)

    c, s = own_turn(32 * lax.div(lane, 64) + lax.rem(lane, 32))
    turn_f[0], turn_f[1] = c, -s
    for load in loads[:4]:
        load.wait()

    def rows_forward(g, first, last):
        for pair in range(first, last, 2):
            cols = []
            for cs in (pair, pair + 1):
                a = a_ref[g, pl.ds(cs, 64, stride=8), :].astype(F32)
                b = b_ref[g, pl.ds(cs, 64, stride=8), :].astype(F32)
                lo = jnp.where(left[:64], a, pltpu.roll(b, 64, 1))
                hi = jnp.where(left[:64], pltpu.roll(a, 64, 1), b)
                cols.append(jnp.concatenate([lo, hi], 0).astype(BF16))
            u_in = jnp.concatenate(cols, 1)
            u = dot(mats[0], jnp.concatenate([u_in, u_in], 0))
            rows = []
            for i in range(2):
                v = times((u[:128, 128 * i : 128 * i + 128], u[128:, 128 * i : 128 * i + 128]), tw(0))
                rows.append(jnp.concatenate(v, 1))
            vh, vl = halves(jnp.concatenate(rows, 0))
            f = dot(vh, mats[1]) + dot(vl, mats[1]) + dot(vh, mats[2])
            r = []
            for i in range(2):
                t = (turn_f[0], turn_f[1])
                r.append(times((f[128 * i : 128 * i + 128, :128], f[128 * i : 128 * i + 128, 128:]), t))
                turn_f[0], turn_f[1] = times(t, tw(1))
            at = 4 * g + pair // 2
            for i in range(2):
                sent[at, i] = jnp.where(left, r[0][i], pltpu.roll(r[1][i], 64, 1))
                sent[PAIRS + at, i] = jnp.where(left, pltpu.roll(r[0][i], 64, 1), r[1][i])

    def forward(g, _):
        rows_forward(g, 0, 8)
        scatter(sent, got, 4 * g, 4, send_f, recv_f.at[g])
        return 0

    rows_forward(0, 0, 4)
    pl.semaphore_wait(barrier, DEV - 1)
    scatter(sent, got, 0, 2, send_f, recv_f.at[8])
    for load in loads[4:]:
        load.wait()
    rows_forward(0, 4, 8)
    scatter(sent, got, 2, 2, send_f, recv_f.at[0])
    lax.fori_loop(1, 4, forward, 0)

    scatter(sent, got, PAIRS, 4, send_f, recv_f.at[4])

    lane8 = lax.broadcasted_iota(jnp.int32, (8, 128), 1)
    left8 = lane8 < 64
    low8 = lax.rem(lane8, 64) < 32
    sign1 = jnp.where(left8, 1.0, -1.0).astype(F32)
    sign2 = jnp.where(low8, 1.0, -1.0).astype(F32)

    def columns(h, _):
        turn_d[0], turn_d[1] = tw(2)

        def devices_digit(g, _):
            first = PAIRS * h + 4 * g
            start = jnp.logical_and(h == 0, g == 0)

            @pl.when(start)
            def _():
                arrived(sent, got, 0, 2, recv_f.at[8])
                arrived(sent, got, 2, 2, recv_f.at[0])

            @pl.when(jnp.logical_not(start))
            def _():
                arrived(sent, got, first, 4, recv_f.at[4 * h + g])

            x_in = jnp.concatenate([got[first + i].reshape(256, 128) for i in range(4)], 1)
            xh, xl = halves(x_in)
            f = dot(mats[3], xh) + dot(mats[3], xl) + dot(mats[4], xh)
            for i in range(4):
                t = (turn_d[0], turn_d[1])
                r = times((f[:128, 128 * i : 128 * i + 128], f[128:, 128 * i : 128 * i + 128]), t)
                mid[4 * g + i, 0] = r[0]
                mid[4 * g + i, 1] = r[1]
                turn_d[0], turn_d[1] = times(t, tw(3))

            @pl.when(jnp.logical_and(h == 0, g < 3))
            def _():
                scatter(sent, got, PAIRS + 4 * (g + 1), 4, send_f, recv_f.at[5 + g])

            return 0

        lax.fori_loop(0, 4, devices_digit, 0)

        def product(t, _):
            rows = pl.ds(pl.multiple_of(8 * t, 8), 8)
            bins = small_dft([(mid[i, 0, rows, :], mid[i, 1, rows, :]) for i in range(PAIRS)], -1)
            folded = []
            for i, v in enumerate(bins):
                w = (vecs[16, pl.ds(i, 1), :], vecs[17, pl.ds(i, 1), :])
                v = times(v, w)
                v = tuple(pltpu.roll(e, 64, 1) + sign1 * e for e in v)
                o = tuple(jnp.where(low8, pltpu.roll(e, 96, 1), pltpu.roll(e, 32, 1)) for e in v)
                p = times(v, o)
                folded.append(tuple(pltpu.roll(e, 64, 1) + sign1 * e for e in p))
            packed = []
            for i in range(8):
                p, q = folded[i], folded[i + 8]
                q = (jnp.where(left8, q[0], -q[1]), jnp.where(left8, q[1], q[0]))
                w = (vecs[18, pl.ds(i, 1), :], vecs[19, pl.ds(i, 1), :])
                packed.append(times((p[0] + sign2 * q[0], p[1] + sign2 * q[1]), w))
            for i, v in enumerate(small_dft(packed, 1)):
                quot[i, 0, rows, :] = v[0]
                quot[i, 1, rows, :] = v[1]
            return 0

        lax.fori_loop(0, 16, product, 0)

        turn_d[0], turn_d[1] = tw(4)

        def devices_back(g, _):
            cols = []
            for i in range(4):
                t = (turn_d[0], turn_d[1])
                r = times((quot[4 * g + i, 0], quot[4 * g + i, 1]), t)
                cols.append(jnp.concatenate(r, 0))
                turn_d[0], turn_d[1] = times(t, tw(5))
            xh, xl = halves(jnp.concatenate(cols, 1))
            f = dot(mats[5], xh) + dot(mats[5], xl) + dot(mats[6], xh)
            first = 8 * h + 4 * g
            for i in range(4):
                back[first + i, 0] = f[:128, 128 * i : 128 * i + 128]
                back[first + i, 1] = f[128:, 128 * i : 128 * i + 128]
            scatter(back, home, first, 2, send_i, recv_i.at[4 * h + 2 * g])
            scatter(back, home, first + 2, 2, send_i, recv_i.at[4 * h + 2 * g + 1])
            return 0

        lax.fori_loop(0, 2, devices_back, 0)
        return 0

    lax.fori_loop(0, HALVES, columns, 0)

    turn_f[0], turn_f[1] = times(own_turn(lax.rem(lane, 64)), tw(7))

    def inverse(g, _):
        arrived(back, home, 2 * g, 2, recv_i.at[g])
        arrived(back, home, 8 + 2 * g, 2, recv_i.at[4 + g])

        for pair in range(2):
            at = 2 * g + pair
            both = ([], [])
            for i in range(2):
                p, q = home[at, i], home[8 + at, i]
                both[0].append(jnp.where(low32, p, pltpu.roll(q, 32, 1)))
                both[1].append(jnp.where(low32, pltpu.roll(p, 96, 1), q))
            rows = []
            for v in both:
                t = (turn_f[0], turn_f[1])
                rows.append(jnp.concatenate(times(v, t), 1))
                turn_f[0], turn_f[1] = times(t, tw(6))
            xh, xl = halves(jnp.concatenate(rows, 0))
            v = dot(xh, mats[7]) + dot(xl, mats[7]) + dot(xh, mats[8])
            c, s = tw(0)
            cols = []
            for i in range(2):
                vi = times((v[128 * i : 128 * i + 128, :128], v[128 * i : 128 * i + 128, 128:]), (c, -s))
                cols.append(jnp.concatenate(vi, 0))
            vh, vl = halves(jnp.concatenate(cols, 1))
            o = dot(mats[9], vh) + dot(mats[9], vl) + dot(mats[10], vh)
            for i in range(2):
                o0, o1 = o[:128, 128 * i : 128 * i + 128], o[128:, 128 * i : 128 * i + 128]
                cs = 4 * pair + 2 * i
                out_ref[g, pl.ds(cs, 128, stride=8), :] = jnp.where(left, o0, pltpu.roll(o1, 64, 1))
                out_ref[g, pl.ds(cs + 1, 128, stride=8), :] = jnp.where(left, pltpu.roll(o0, 64, 1), o1)
        return 0

    lax.fori_loop(0, 4, inverse, 0)
    all_sent(sent, got, send_f)
    all_sent(back, home, send_i)


def on_device(limbs_a, limbs_b):
    def tiles(x):
        return x.reshape(4, 8, 64, 128).transpose(0, 2, 1, 3).reshape(4, 512, 128)

    out = pl.pallas_call(
        kernel,
        out_shape=pltpu.VMEM((4, 1024, 128), F32),
        in_specs=[pl.BlockSpec(memory_space=pltpu.HBM)] * 4,
        out_specs=pl.BlockSpec(memory_space=pltpu.VMEM),
        scratch_shapes=[
            pltpu.VMEM((4, 512, 128), jnp.int32),
            pltpu.VMEM((4, 512, 128), jnp.int32),
            pltpu.VMEM((11, 256, 256), BF16),
            pltpu.VMEM((20, 128, 128), F32),
            pltpu.VMEM((LOCAL, 2, 128, 128), F32),
            pltpu.VMEM((LOCAL, 2, 128, 128), F32),
            pltpu.VMEM((PAIRS, 2, 128, 128), F32),
            pltpu.VMEM((8, 2, 128, 128), F32),
            pltpu.VMEM((16, 2, 128, 128), F32),
            pltpu.VMEM((16, 2, 128, 128), F32),
            pltpu.VMEM((2, 128, 128), F32),
            pltpu.VMEM((2, 128, 128), F32),
            pltpu.SemaphoreType.DMA((8,)),
            pltpu.SemaphoreType.DMA,
            pltpu.SemaphoreType.DMA((9,)),
            pltpu.SemaphoreType.DMA,
            pltpu.SemaphoreType.DMA((8,)),
        ],
        compiler_params=pltpu.CompilerParams(
            collective_id=0, has_side_effects=True, vmem_limit_bytes=60 << 20
        ),
    )(tiles(limbs_a), tiles(limbs_b), jnp.asarray(matrix_tables()), jnp.asarray(vector_tables()))
    return out.reshape(4, 128, 8, 128).transpose(0, 2, 1, 3).reshape(LOCAL, ROWS)


def solution(mesh):
    placed = (P(("fft", "grp"), None), P(("fft", "grp"), None))
    return jax.shard_map(
        on_device, mesh=mesh, in_specs=placed, out_specs=P(("fft", "grp"), None), check_vma=False
    )
```

```python
import functools
import math

import jax
import jax.numpy as jnp
import ml_dtypes
import numpy as np
from jax import lax
from jax.experimental import pallas as pl
from jax.experimental.pallas import tpu as pltpu
from jax.sharding import PartitionSpec as P

MESH = pl.DeviceIdType.MESH
ROWS = 16384
COLS = 4096
TOTAL = ROWS * COLS
DIGIT_VAR = 5461.25
DEV = 128
LOCAL = COLS // DEV
HALVES = 2
PAIRS = LOCAL // 2
FWD_CHUNKS = 4
INV_CHUNKS = 2
F32 = jnp.float32
BF16 = jnp.bfloat16


def turn(num, den):
    angle = (np.asarray(num, np.int64) % den) * (2.0 * math.pi / den)
    return np.cos(angle), np.sin(angle)


def split_pair(table):
    high = table.astype(ml_dtypes.bfloat16)
    low = (table - high.astype(np.float64)).astype(ml_dtypes.bfloat16)
    return high, low


@functools.lru_cache(None)
def matrix_tables():
    ka = np.arange(128)
    lane = np.arange(64)
    order = np.concatenate([2 * np.arange(64), 2 * np.arange(64) + 1])
    c, s = turn(np.outer(2 * ka + 1, order), 512)
    first = split_pair(np.concatenate([c, -s], 0))
    first = np.concatenate([first[0], first[1]], 1)
    c, s = turn(np.outer(lane, lane), 64)
    z = np.zeros_like(c)
    c2, s2 = np.block([[c, z], [z, c]]), np.block([[s, z], [z, s]])
    lanes_inv = split_pair(np.block([[c2, s2], [-s2, c2]]))
    at = np.arange(128)
    at = at // 64 * 32 + at % 64 // 32 * 64 + at % 32
    c2, s2 = c2[:, at], s2[:, at]
    lanes_fwd = split_pair(np.block([[c2, -s2], [s2, c2]]))
    c, s = turn(np.outer(ka, ka), 128)
    dev_fwd = split_pair(np.block([[c, s], [-s, c]]))
    dev_inv = split_pair(np.block([[c, -s], [s, c]]))
    scale = 2.0 / (TOTAL * DIGIT_VAR * math.sqrt(TOTAL // 2))
    order = np.concatenate([2 * np.arange(128), 2 * np.arange(128) + 1])
    c, s = turn(np.outer(order, 2 * ka + 1), 512)
    last = split_pair(np.concatenate([c, -s], 1) * scale)
    mats = [first, *lanes_fwd, *dev_fwd, *dev_inv, *lanes_inv, *last]
    return np.stack(mats)


@functools.lru_cache(None)
def vector_tables():
    ka = np.arange(128)[:, None]
    lane = np.arange(128)[None, :]
    low, par = lane % 64, lane // 64
    two = par + 2 * (lane % 64 // 32)
    zero = 0 * lane
    k1 = ka + 256 * low
    k1_sent = ka + 256 * (32 * par + lane % 32)
    pairs = [
        turn(-low * (2 * ka + 1), 2 * ROWS),
        turn(-(2 * k1_sent + 1), 2 * TOTAL),
        turn(-ka * par, COLS),
        turn(-2 * ka + zero, COLS),
        turn(ka * two, COLS),
        turn(4 * ka + zero, COLS),
        turn(2 * (2 * k1 + 1), 2 * TOTAL),
        turn(par * (2 * k1 + 1), 2 * TOTAL),
        turn(-ka * par, 32),
        turn(ka * two, 32),
    ]
    return np.stack([t for pair in pairs for t in pair]).astype(np.float32)


def all_displacements():
    out = []
    for i in range(16):
        for j in range(8):
            dx, dy = i // 4 + j + j // 4, i % 4 + 2 * j + j // 2
            out.append((dx % 4, dy % 4, j % 4, j // 4))
    return out[1:]


PEERS = all_displacements()


def hops(place):
    return sum(min(v, 4 - v) for v in place[:3])


def times(a, b):
    return a[0] * b[0] - a[1] * b[1], a[0] * b[1] + a[1] * b[0]


def turned(value, num, den):
    num %= den
    re, im = value
    if num == 0:
        return value
    if 4 * num == den:
        return -im, re
    if 2 * num == den:
        return -re, -im
    if 4 * num == 3 * den:
        return im, -re
    c, s = math.cos(2 * math.pi * num / den), math.sin(2 * math.pi * num / den)
    if 8 * num % den == 0:
        root = math.sqrt(0.5)
        sc, ss = math.copysign(1.0, c), math.copysign(1.0, s)
        first = re if sc > 0 else -re
        first = first - im if ss > 0 else first + im
        second = re if ss > 0 else -re
        second = second + im if sc > 0 else second - im
        return first * root, second * root
    return re * c - im * s, re * s + im * c


def small_dft(values, sign):
    n = len(values)
    if n == 1:
        return values
    half = n // 2
    even = [(a[0] + b[0], a[1] + b[1]) for a, b in zip(values[:half], values[half:])]
    odd = [
        turned((a[0] - b[0], a[1] - b[1]), sign * i, n)
        for i, (a, b) in enumerate(zip(values[:half], values[half:]))
    ]
    even, odd = small_dft(even, sign), small_dft(odd, sign)
    return [v for pair in zip(even, odd) for v in pair]


def halves(value):
    high = value.astype(BF16)
    return high, (value - high.astype(F32)).astype(BF16)


def dot(a, b):
    return jnp.dot(a, b, preferred_element_type=F32)


def kernel(
    a_hbm, b_hbm, mats_hbm, vecs_hbm, out_ref,
    a_ref, b_ref, mats, vecs, sent, got, mid, quot, back, home, turn_f, turn_d,
    in_sem, send_f, recv_f, send_i, recv_i,
):
    fft, grp = lax.axis_index("fft"), lax.axis_index("grp")
    me = fft * 2 + grp
    barrier = pltpu.get_barrier_semaphore()

    parts = [(a_hbm, a_ref, 0, 1), (b_hbm, b_ref, 0, 1), (mats_hbm, mats, 0, 3), (vecs_hbm, vecs, 0, 4)]
    parts += [(a_hbm, a_ref, 1, 3), (b_hbm, b_ref, 1, 3), (mats_hbm, mats, 3, 8), (vecs_hbm, vecs, 4, 16)]
    loads = [
        pltpu.make_async_copy(src.at[pl.ds(at, n)], dst.at[pl.ds(at, n)], in_sem.at[i])
        for i, (src, dst, at, n) in enumerate(parts)
    ]
    for load in loads:
        load.start()

    core, z, x = lax.rem(fft, 2), lax.rem(lax.div(fft, 2), 4), lax.rem(lax.div(fft, 8), 4)
    y = lax.div(fft, 32) * 2 + grp
    cores = [core, 1 - core]
    zs = [lax.rem(z + t, 4) * 2 for t in range(4)]
    xs = [lax.rem(x + t, 4) * 8 for t in range(4)]
    ys = [lax.rem(y + t, 4) for t in range(4)]
    highs = [lax.div(v, 2) * 32 for v in ys]
    lows = [lax.rem(v, 2) for v in ys]

    def peer_at(dx, dy, dz, dc):
        return highs[dy] + xs[dx] + zs[dz] + cores[dc], lows[dy]

    def signal(sem, place):
        pl.semaphore_signal(sem, inc=1, device_id=peer_at(*place), device_id_type=MESH)

    for place in sorted(PEERS, key=lambda d: -hops(d)):
        signal(barrier, place)

    def send(src, dst, part, place, send_sem, recv_sem):
        peer = peer_at(*place)
        pltpu.make_async_remote_copy(
            src_ref=src.at[part, :, pl.ds(peer[0] * 2 + peer[1], 1)],
            dst_ref=dst.at[part, :, pl.ds(me, 1)],
            send_sem=send_sem,
            recv_sem=recv_sem,
            device_id=peer,
            device_id_type=MESH,
        ).start()

    def scatter(src, dst, first, count, send_sem, recv_sem, places=PEERS):
        part = pl.ds(first, count)
        own = pl.ds(me, 1)
        pltpu.make_async_copy(src.at[part, :, own], dst.at[part, :, own], recv_sem).start()

        for place in places:
            send(src, dst, part, place, send_sem, recv_sem)

    def arrived(src, dst, first, count, recv_sem):
        part = pl.ds(first, count)
        pltpu.make_async_copy(src.at[part], dst.at[part], recv_sem).wait()

    def all_sent(src, dst, send_sem):
        part = pl.ds(0, DEV - 1)
        pltpu.make_async_copy(src.at[:, :, part], dst.at[:, :, part], send_sem).wait()

    row = lax.broadcasted_iota(jnp.int32, (128, 128), 0)
    lane = lax.broadcasted_iota(jnp.int32, (128, 128), 1)
    left = lane < 64
    low32 = lax.rem(lane, 64) < 32
    tw = lambda i: (vecs[2 * i], vecs[2 * i + 1])

    def own_turn(kb):
        angle = (me * (2 * (row + 256 * kb) + 1)).astype(F32)
        angle = angle * (2.0 * math.pi / (2 * TOTAL // LOCAL))
        return jnp.cos(angle), jnp.sin(angle)

    c, s = own_turn(32 * lax.div(lane, 64) + lax.rem(lane, 32))
    turn_f[0], turn_f[1] = c, -s
    for load in loads[:4]:
        load.wait()

    def rows_forward(g, first, last):
        for pair in range(first, last, 2):
            cols = []
            for cs in (pair, pair + 1):
                a = a_ref[g, pl.ds(cs, 64, stride=8), :].astype(F32)
                b = b_ref[g, pl.ds(cs, 64, stride=8), :].astype(F32)
                lo = jnp.where(left[:64], a, pltpu.roll(b, 64, 1))
                hi = jnp.where(left[:64], pltpu.roll(a, 64, 1), b)
                cols.append(jnp.concatenate([lo, hi], 0).astype(BF16))
            u_in = jnp.concatenate(cols, 1)
            u = dot(mats[0], jnp.concatenate([u_in, u_in], 0))
            rows = []
            for i in range(2):
                v = times((u[:128, 128 * i : 128 * i + 128], u[128:, 128 * i : 128 * i + 128]), tw(0))
                rows.append(jnp.concatenate(v, 1))
            vh, vl = halves(jnp.concatenate(rows, 0))
            f = dot(vh, mats[1]) + dot(vl, mats[1]) + dot(vh, mats[2])
            r = []
            for i in range(2):
                t = (turn_f[0], turn_f[1])
                r.append(times((f[128 * i : 128 * i + 128, :128], f[128 * i : 128 * i + 128, 128:]), t))
                turn_f[0], turn_f[1] = times(t, tw(1))
            at = 4 * g + pair // 2
            for i in range(2):
                sent[at, i] = jnp.where(left, r[0][i], pltpu.roll(r[1][i], 64, 1))
                sent[PAIRS + at, i] = jnp.where(left, pltpu.roll(r[0][i], 64, 1), r[1][i])

    def forward(g, _):
        rows_forward(g, 0, 8)
        scatter(sent, got, 4 * g, 4, send_f, recv_f.at[g])
        return 0

    rows_forward(0, 0, 4)
    pl.semaphore_wait(barrier, DEV - 1)
    scatter(sent, got, 0, 2, send_f, recv_f.at[8])
    for load in loads[4:]:
        load.wait()
    rows_forward(0, 4, 8)
    scatter(sent, got, 2, 2, send_f, recv_f.at[0])
    lax.fori_loop(1, 4, forward, 0)

    scatter(sent, got, PAIRS, 4, send_f, recv_f.at[4])

    lane8 = lax.broadcasted_iota(jnp.int32, (8, 128), 1)
    left8 = lane8 < 64
    low8 = lax.rem(lane8, 64) < 32
    sign1 = jnp.where(left8, 1.0, -1.0).astype(F32)
    sign2 = jnp.where(low8, 1.0, -1.0).astype(F32)

    def columns(h, _):
        turn_d[0], turn_d[1] = tw(2)

        def devices_digit(g, _):
            first = PAIRS * h + 4 * g
            start = jnp.logical_and(h == 0, g == 0)

            @pl.when(start)
            def _():
                arrived(sent, got, 0, 2, recv_f.at[8])
                arrived(sent, got, 2, 2, recv_f.at[0])

            @pl.when(jnp.logical_not(start))
            def _():
                arrived(sent, got, first, 4, recv_f.at[4 * h + g])

            x_in = jnp.concatenate([got[first + i].reshape(256, 128) for i in range(4)], 1)
            xh, xl = halves(x_in)
            f = dot(mats[3], xh) + dot(mats[3], xl) + dot(mats[4], xh)
            for i in range(4):
                t = (turn_d[0], turn_d[1])
                r = times((f[:128, 128 * i : 128 * i + 128], f[128:, 128 * i : 128 * i + 128]), t)
                mid[4 * g + i, 0] = r[0]
                mid[4 * g + i, 1] = r[1]
                turn_d[0], turn_d[1] = times(t, tw(3))

            @pl.when(jnp.logical_and(h == 0, g < 3))
            def _():
                scatter(sent, got, PAIRS + 4 * (g + 1), 4, send_f, recv_f.at[5 + g])

            return 0

        lax.fori_loop(0, 4, devices_digit, 0)

        def product(t, _):
            rows = pl.ds(pl.multiple_of(8 * t, 8), 8)
            bins = small_dft([(mid[i, 0, rows, :], mid[i, 1, rows, :]) for i in range(PAIRS)], -1)
            folded = []
            for i, v in enumerate(bins):
                w = (vecs[16, pl.ds(i, 1), :], vecs[17, pl.ds(i, 1), :])
                v = times(v, w)
                v = tuple(pltpu.roll(e, 64, 1) + sign1 * e for e in v)
                o = tuple(jnp.where(low8, pltpu.roll(e, 96, 1), pltpu.roll(e, 32, 1)) for e in v)
                p = times(v, o)
                folded.append(tuple(pltpu.roll(e, 64, 1) + sign1 * e for e in p))
            packed = []
            for i in range(8):
                p, q = folded[i], folded[i + 8]
                q = (jnp.where(left8, q[0], -q[1]), jnp.where(left8, q[1], q[0]))
                w = (vecs[18, pl.ds(i, 1), :], vecs[19, pl.ds(i, 1), :])
                packed.append(times((p[0] + sign2 * q[0], p[1] + sign2 * q[1]), w))
            for i, v in enumerate(small_dft(packed, 1)):
                quot[i, 0, rows, :] = v[0]
                quot[i, 1, rows, :] = v[1]
            return 0

        lax.fori_loop(0, 16, product, 0)

        turn_d[0], turn_d[1] = tw(4)

        def devices_back(g, _):
            cols = []
            for i in range(4):
                t = (turn_d[0], turn_d[1])
                r = times((quot[4 * g + i, 0], quot[4 * g + i, 1]), t)
                cols.append(jnp.concatenate(r, 0))
                turn_d[0], turn_d[1] = times(t, tw(5))
            xh, xl = halves(jnp.concatenate(cols, 1))
            f = dot(mats[5], xh) + dot(mats[5], xl) + dot(mats[6], xh)
            first = 8 * h + 4 * g
            for i in range(4):
                back[first + i, 0] = f[:128, 128 * i : 128 * i + 128]
                back[first + i, 1] = f[128:, 128 * i : 128 * i + 128]
            scatter(back, home, first, 2, send_i, recv_i.at[4 * h + 2 * g])
            scatter(back, home, first + 2, 2, send_i, recv_i.at[4 * h + 2 * g + 1], sorted(PEERS, key=lambda d: -hops(d)))
            return 0

        lax.fori_loop(0, 2, devices_back, 0)
        return 0

    lax.fori_loop(0, HALVES, columns, 0)

    turn_f[0], turn_f[1] = times(own_turn(lax.rem(lane, 64)), tw(7))

    def inverse(g, _):
        arrived(back, home, 2 * g, 2, recv_i.at[g])
        arrived(back, home, 8 + 2 * g, 2, recv_i.at[4 + g])

        for pair in range(2):
            at = 2 * g + pair
            both = ([], [])
            for i in range(2):
                p, q = home[at, i], home[8 + at, i]
                both[0].append(jnp.where(low32, p, pltpu.roll(q, 32, 1)))
                both[1].append(jnp.where(low32, pltpu.roll(p, 96, 1), q))
            rows = []
            for v in both:
                t = (turn_f[0], turn_f[1])
                rows.append(jnp.concatenate(times(v, t), 1))
                turn_f[0], turn_f[1] = times(t, tw(6))
            xh, xl = halves(jnp.concatenate(rows, 0))
            v = dot(xh, mats[7]) + dot(xl, mats[7]) + dot(xh, mats[8])
            c, s = tw(0)
            cols = []
            for i in range(2):
                vi = times((v[128 * i : 128 * i + 128, :128], v[128 * i : 128 * i + 128, 128:]), (c, -s))
                cols.append(jnp.concatenate(vi, 0))
            vh, vl = halves(jnp.concatenate(cols, 1))
            o = dot(mats[9], vh) + dot(mats[9], vl) + dot(mats[10], vh)
            for i in range(2):
                o0, o1 = o[:128, 128 * i : 128 * i + 128], o[128:, 128 * i : 128 * i + 128]
                cs = 4 * pair + 2 * i
                out_ref[g, pl.ds(cs, 128, stride=8), :] = jnp.where(left, o0, pltpu.roll(o1, 64, 1))
                out_ref[g, pl.ds(cs + 1, 128, stride=8), :] = jnp.where(left, pltpu.roll(o0, 64, 1), o1)
        return 0

    lax.fori_loop(0, 4, inverse, 0)
    all_sent(sent, got, send_f)
    all_sent(back, home, send_i)


def on_device(limbs_a, limbs_b):
    def tiles(x):
        return x.reshape(4, 8, 64, 128).transpose(0, 2, 1, 3).reshape(4, 512, 128)

    out = pl.pallas_call(
        kernel,
        out_shape=pltpu.VMEM((4, 1024, 128), F32),
        in_specs=[pl.BlockSpec(memory_space=pltpu.HBM)] * 4,
        out_specs=pl.BlockSpec(memory_space=pltpu.VMEM),
        scratch_shapes=[
            pltpu.VMEM((4, 512, 128), jnp.int32),
            pltpu.VMEM((4, 512, 128), jnp.int32),
            pltpu.VMEM((11, 256, 256), BF16),
            pltpu.VMEM((20, 128, 128), F32),
            pltpu.VMEM((LOCAL, 2, 128, 128), F32),
            pltpu.VMEM((LOCAL, 2, 128, 128), F32),
            pltpu.VMEM((PAIRS, 2, 128, 128), F32),
            pltpu.VMEM((8, 2, 128, 128), F32),
            pltpu.VMEM((16, 2, 128, 128), F32),
            pltpu.VMEM((16, 2, 128, 128), F32),
            pltpu.VMEM((2, 128, 128), F32),
            pltpu.VMEM((2, 128, 128), F32),
            pltpu.SemaphoreType.DMA((8,)),
            pltpu.SemaphoreType.DMA,
            pltpu.SemaphoreType.DMA((9,)),
            pltpu.SemaphoreType.DMA,
            pltpu.SemaphoreType.DMA((8,)),
        ],
        compiler_params=pltpu.CompilerParams(
            collective_id=0, has_side_effects=True, vmem_limit_bytes=60 << 20
        ),
    )(tiles(limbs_a), tiles(limbs_b), jnp.asarray(matrix_tables()), jnp.asarray(vector_tables()))
    return out.reshape(4, 128, 8, 128).transpose(0, 2, 1, 3).reshape(LOCAL, ROWS)


def solution(mesh):
    placed = (P(("fft", "grp"), None), P(("fft", "grp"), None))
    return jax.shard_map(
        on_device, mesh=mesh, in_specs=placed, out_specs=P(("fft", "grp"), None), check_vma=False
    )
```
